128 devices in a mesh: blk: 64 (over x, z_lo, y, core), split: 2 (over z_hi).
Axes of the slice: x: 4, y: 4, z: 4 (z_hi: 2, z_lo: 2; z = z_hi * 2 + z_lo), core: 2. Of those that a mesh axis runs over, the one named last changes fastest.
Arguments:
- queries: bfloat16 [64, 512, 1024], P('blk'), may hold values from -54 to 54
- prefix_kv: bfloat16 [16384, 256], P(('blk', 'split')), may hold values from -12 to 12
- suffix_kv: bfloat16 [64, 512, 256], P('blk', 'split'), may hold values from -6 to 6
Outputs:
- attended: bfloat16 [64, 512, 1024], P('blk', None, 'split')
The draws below stay inside these ranges and needn't reach their ends.
All inputs are finite; a program needn't handle non-finite values.
Results may differ from the reference program's by a relative error of at most 0.018.
Values may be sent and summed in bfloat16 or wider, within the bound.
A program may use at most 64 MiB of HBM per device.

```python
import math
import jax
import jax.numpy as jnp
from jax import lax

DH = 128
HEADS = 8
S = 512
SUFFIXES = 64
PREFIX = 16384


def draw_queries(key, part):
    key = jax.random.fold_in(key, 1)
    values = jnp.clip(3.0 * jax.random.normal(key, (SUFFIXES, S, HEADS * DH), jnp.float32), -18.0, 18.0)
    return values.astype(jnp.bfloat16)


def draw_prefix_kv(key, part):
    key = jax.random.fold_in(key, 2)
    key_one, key_two = jax.random.split(key, 2)
    keys_drawn = jnp.clip(jax.random.normal(key_one, (PREFIX, DH), jnp.float32), -6.0, 6.0)
    values_drawn = jnp.clip(jax.random.normal(key_two, (PREFIX, DH), jnp.float32), -6.0, 6.0)
    return jnp.concatenate([keys_drawn, values_drawn], axis=1).astype(jnp.bfloat16)


def levels(rng, extent, pieces, least, top_value):
    def one(axis_at, parts):
        heights = jax.random.uniform(jax.random.fold_in(jax.random.fold_in(rng, 6), axis_at), (parts,), jnp.float32, least / len(pieces), top_value / len(pieces))
        return jnp.repeat(jnp.exp(heights), extent[axis_at] // parts).reshape((-1,) + (1,) * (len(extent) - axis_at - 1))

    loudness = one(*pieces[0])
    for cut in pieces[1:]:
        loudness = loudness * one(*cut)
    return loudness


def gaussian(own_key, dims, spread, reach, shards=(), held_as=jnp.bfloat16):
    gain = levels(own_key, dims, shards, -0.22, 0.18) if shards else 1.0
    values = jax.random.normal(own_key, dims, jnp.float32) * spread * gain
    return jnp.minimum(jnp.maximum(values, -reach), reach).astype(held_as)


def setup_inputs(seed: int = 0) -> dict:
    arg_keys = jax.random.split(jax.random.key(seed), 4)
    queries = draw_queries(jax.random.fold_in(arg_keys[3], 71), 0)
    prefix_kv = draw_prefix_kv(jax.random.fold_in(arg_keys[3], 71), 0)
    suffix_kv = gaussian(arg_keys[2], (SUFFIXES, S, 2 * DH), 1.0, 6.0, ((0, 64), (1, 2)))
    return dict(queries=queries, prefix_kv=prefix_kv, suffix_kv=suffix_kv)


def reference(queries, prefix_kv, suffix_kv):
    scale = 1.0 / math.sqrt(DH)
    prefix_keys = prefix_kv[:, :DH]
    prefix_values = prefix_kv[:, DH:]
    token_pos = (jnp.arange(S * HEADS) // HEADS).astype(jnp.int32)
    allowed = jnp.arange(S).astype(jnp.int32)[None, :] <= token_pos[:, None]

    def per_suffix(pair):
        query_block, own_kv = pair
        query_rows = query_block.reshape(S * HEADS, DH)
        prefix_scores = jnp.dot(query_rows, prefix_keys.T, preferred_element_type=jnp.float32) * scale
        suffix_scores = jnp.dot(query_rows, own_kv[:, :DH].T, preferred_element_type=jnp.float32) * scale
        suffix_scores = jnp.where(allowed, suffix_scores, -1e+30)
        row_max = jnp.maximum(prefix_scores.max(axis=1), suffix_scores.max(axis=1))
        prefix_weights = jnp.exp(prefix_scores - row_max[:, None])
        suffix_weights = jnp.where(allowed, jnp.exp(suffix_scores - row_max[:, None]), 0.0)
        denominator = prefix_weights.sum(axis=1) + suffix_weights.sum(axis=1)
        numerator = jnp.dot(prefix_weights.astype(jnp.bfloat16), prefix_values, preferred_element_type=jnp.float32)
        numerator = numerator + jnp.dot(suffix_weights.astype(jnp.bfloat16), own_kv[:, DH:], preferred_element_type=jnp.float32)
        return (numerator / denominator[:, None]).reshape(S, HEADS * DH).astype(jnp.bfloat16)
    return lax.map(per_suffix, (queries, suffix_kv))
```

```python
import functools
import math

import jax
import jax.numpy as jnp
from jax import lax
from jax.experimental import pallas as pl
from jax.experimental.pallas import tpu as pltpu
from jax.sharding import PartitionSpec as P

MESH = pl.DeviceIdType.MESH
D = 128
SUB = 8
LANES = 256
LINE = 4
BLOCK = 128
TOKENS = 2 * LINE * BLOCK
PIECES = 4
PIECE = TOKENS // PIECES
LOG2E = 1.4426950408889634
NEG = -1e30


def gray(i):
    return i + (i // 2) * (1 - 2 * (i % 2))


def kernel(
    q_hbm, prefix_ref, suffix_ref, out_ref,
    kv, q_in, q_t, other, s0, s1, p0, p1, x0, x1, c0, c1, m_ref, l_ref, acc,
    q_sem, send_sem, recv_sem, line_sem, sib_sem,
):
    scale = LOG2E / math.sqrt(D)
    scores, weights, tops, fixes = (s0, s1), (p0, p1), (x0, x1), (c0, c1)
    tokens_here = suffix_ref.shape[1]
    seq, width = q_in.shape
    heads = width // D
    rows = heads * seq
    units = rows // LANES

    blk, split = lax.axis_index("blk"), lax.axis_index("split")
    core = blk % 2
    x, y, z = blk // 16, (blk // 2) % 4, split * 2 + (blk // 8) % 2

    def device(d1=0, d2=0, d3=0, other_core=0):
        nx = (x + d1 * (1 - core) + d3 * core) % 4
        ny = (y + d2) % 4
        nz = (z + d1 * core + d3 * (1 - core)) % 4
        nc = (core + other_core) % 2
        return (nx * 16 + (nz % 2) * 8 + ny * 2 + nc, nz // 2)

    a1 = x * (1 - core) + z * core
    a3 = z * (1 - core) + x * core
    sibling = device(other_core=1)
    partner = ((x * 16 + (z % 2) * 8 + y * 2 + core), 1 - split)
    peers = [device(d1=1), device(d1=2), device(d1=3), device(d2=1), device(d2=3), device(d3=1), device(d3=3)]

    barrier = pltpu.get_barrier_semaphore()
    for peer in peers + [sibling, partner]:
        pl.semaphore_signal(barrier, inc=1, device_id=peer, device_id_type=MESH)

    q_copy = pltpu.make_async_copy(
        q_hbm.at[0, :, pl.ds(pl.multiple_of(split * width, width), width)], q_in, q_sem
    )
    q_copy.start()

    kv[core, a3, y, a1, 0] = prefix_ref[:, :D]
    kv[core, a3, y, a1, 1] = prefix_ref[:, D:].astype(jnp.float32).T.astype(jnp.bfloat16)

    m_ref[...] = jnp.full_like(m_ref, NEG)
    l_ref[...] = jnp.zeros_like(l_ref)
    acc[...] = jnp.zeros_like(acc)
    p1[...] = jnp.zeros_like(p1)
    c1[...] = jnp.ones_like(c1)

    pl.semaphore_wait(barrier, 9)

    def remote(src, dst, send, recv, target):
        return pltpu.make_async_remote_copy(
            src_ref=src, dst_ref=dst, send_sem=send, recv_sem=recv, device_id=target, device_id_type=MESH
        )

    def first(d):
        here = kv.at[core, a3, y, a1]
        return remote(here, here, send_sem.at[d - 1], recv_sem.at[3 - d], device(d1=d))

    def line_at(d3, d2):
        return kv.at[core, (a3 + d3) % 4, (y + d2) % 4]

    sends = []

    def line_copy(index, d3, d2, s3, s2):
        ref = line_at(d3, d2)
        landing = ((d3 - s3) % 4) * 4 + (d2 - s2) % 4
        return remote(ref, ref, send_sem.at[3 + index], line_sem.at[landing], device(d3=s3 % 4, d2=s2 % 4))

    def sib_copy(d3, d2):
        ref = line_at(d3, d2)
        return remote(ref, ref, send_sem.at[19 + d3 * 4 + d2], sib_sem.at[d3 * 4 + d2], sibling)

    def other_copy():
        return remote(suffix_ref.at[0], other, send_sem.at[18], recv_sem.at[3], partner)

    plan = [
        (0, 0, 0, 1), (0, 0, 0, -1), (0, 3, 0, 1),
        (0, 0, 1, 0), (0, 0, -1, 0), (0, 1, 1, 0), (0, 1, -1, 0),
        (0, 3, 1, 0), (0, 3, -1, 0), (0, 2, 1, 0), (0, 2, -1, 0),
        (3, 0, 1, 0), (3, 1, 1, 0), (1, 2, -1, 0), (1, 3, -1, 0),
    ]

    def event(d3, d2):
        if (d3, d2) == (0, 0):
            for d in (1, 2, 3):
                first(d).wait_recv()
        else:
            ref = line_at(d3, d2)
            remote(ref, ref, send_sem.at[3], line_sem.at[d3 * 4 + d2], sibling).wait_recv()
        for index, (e3, e2, s3, s2) in enumerate(plan):
            if (e3, e2) == (d3, d2):
                line_copy(index, e3, e2, s3, s2).start()
        sib_copy(d3, d2).start()

    def sib_wait(d3, d2):
        ref = kv.at[1 - core, (a1 + d3) % 4, (y + d2) % 4]
        remote(ref, ref, send_sem.at[3], sib_sem.at[d3 * 4 + d2], sibling).wait_recv()

    for d in (1, 2, 3):
        first(d).start()
    other_copy().start()

    q_copy.wait()
    for h in range(heads):
        q_t[:, h * seq : (h + 1) * seq] = q_in[:, h * D : (h + 1) * D].astype(jnp.float32).T.astype(jnp.bfloat16)

    def cols(b):
        return slice(b * LANES, (b + 1) * LANES)

    def tile_max(s):
        return jnp.max(s.reshape(s.shape[0] // SUB, SUB, LANES), axis=0)

    def own_part(keys, values_t, offset):
        for b in range(units):
            s = jnp.dot(keys, q_t[:, cols(b)], preferred_element_type=jnp.float32)
            u = lax.broadcasted_iota(jnp.int32, s.shape, 0) + offset
            t = lax.broadcasted_iota(jnp.int32, s.shape, 1) + (b * LANES) % seq
            s = jnp.where(u <= t, s, NEG)
            m_old = m_ref[:, cols(b)]
            m_new = jnp.maximum(m_old, jnp.max(tile_max(s), axis=0, keepdims=True) * scale)
            fix = jnp.exp2(m_old - m_new)
            m_ref[:, cols(b)] = m_new
            p = jnp.exp2(s * scale - m_new)
            l_ref[:, cols(b)] = l_ref[:, cols(b)] * fix + jnp.sum(p.reshape(-1, SUB, LANES), axis=0)
            acc[:, cols(b)] = acc[:, cols(b)] * fix + jnp.dot(
                values_t, p.astype(jnp.bfloat16), preferred_element_type=jnp.float32
            )

    def values_of(ref):
        return ref[:, D:].astype(jnp.float32).T.astype(jnp.bfloat16)

    own_part(suffix_ref[0, :, :D], values_of(suffix_ref.at[0]), split * tokens_here)

    def lines(i):
        d3, d2 = gray(i // 4), gray(i % 4)
        return (core, (a3 + d3) % 4, (y + d2) % 4), (1 - core, (a1 + d3) % 4, (y + d2) % 4)

    def keys_of(i, j):
        c, l3, l2 = lines(i)[j // 2]
        k = 2 * (j % 2)
        return kv[c, l3, l2, pl.ds(k, 2), 0].reshape(PIECE, D)

    def qk(i, b, buf, j, top):
        s = jnp.dot(keys_of(i, j), q_t[:, cols(b)], preferred_element_type=jnp.float32)
        scores[buf][j * PIECE : (j + 1) * PIECE, :] = s
        here = tile_max(s)
        return here if top is None else jnp.maximum(top, here)

    def pv(i, buf):
        parts = []
        for c, l3, l2 in lines(i):
            parts += [kv[c, l3, l2, k, 1] for k in range(LINE)]
        return jnp.dot(jnp.concatenate(parts, axis=1), weights[buf][...], preferred_element_type=jnp.float32)

    last = 15

    def unit(i, b):
        ni, nb = (i, b + 1) if b < units - 1 else (jnp.minimum(i + 1, last), 0)
        pi, pb = (i, b - 1) if b > 0 else (jnp.maximum(i - 1, 0), units - 1)
        buf, nbuf = b % 2, (b + 1) % 2
        m_old = m_ref[:, cols(b)]
        m_new = jnp.maximum(m_old, jnp.max(tops[buf][...], axis=0, keepdims=True) * scale)
        fix = jnp.exp2(m_old - m_new)
        m_ref[:, cols(b)] = m_new
        fixes[buf][...] = fix
        total = l_ref[:, cols(b)] * fix
        top, add = None, None
        for j in range(PIECES):
            top = qk(ni, nb, nbuf, j, top)
            if j == 0:
                add = pv(pi, nbuf)
            part = slice(j * PIECE, (j + 1) * PIECE)
            p = jnp.exp2(scores[buf][part, :] * scale - m_new)
            weights[buf][part, :] = p.astype(jnp.bfloat16)
            total = total + jnp.sum(p.reshape(-1, SUB, LANES), axis=0)
        tops[nbuf][...] = top
        l_ref[:, cols(b)] = total
        acc[:, cols(pb)] = acc[:, cols(pb)] * fixes[nbuf][...] + add

    handed = {
        0: [(0, 3), (0, 1), (3, 0), (1, 0)],
        1: [(3, 1), (1, 3), (3, 3), (1, 1)],
        2: [(0, 2), (2, 0)],
        3: [(3, 2), (1, 2)],
        4: [(2, 1), (2, 3)],
        5: [(2, 2)],
    }

    event(0, 0)
    sib_wait(0, 0)
    top = None
    for j in range(PIECES):
        top = qk(0, 0, 0, j, top)
    tops[0][...] = top

    def body(i, carry):
        for b in range(units):
            if b == units // 2:
                for step, group in handed.items():
                    @pl.when(i == step)
                    def _(group=group):
                        for d3, d2 in group:
                            event(d3, d2)
            if b == units - 1:
                for step in range(1, 16):
                    @pl.when(i + 1 == step)
                    def _(step=step):
                        sib_wait(gray(step // 4), gray(step % 4))
            unit(i, b)
        return carry

    lax.fori_loop(0, 16, body, 0)
    pb = units - 1
    acc[:, cols(pb)] = acc[:, cols(pb)] * fixes[pb % 2][...] + pv(last, pb % 2)

    other_copy().wait_recv()
    own_part(other[:, :D], values_of(other), (1 - split) * tokens_here)

    for h in range(heads):
        part = slice(h * seq, (h + 1) * seq)
        inverse = 1.0 / jnp.sum(l_ref[:, part], axis=0, keepdims=True)
        out_ref[0, :, h * D : (h + 1) * D] = (acc[:, part] * inverse).T.astype(jnp.bfloat16)

    for d in (1, 2, 3):
        first(d).wait_send()
    other_copy().wait_send()
    for index, (e3, e2, s3, s2) in enumerate(plan):
        line_copy(index, e3, e2, s3, s2).wait_send()
    for d3 in range(4):
        for d2 in range(4):
            sib_copy(d3, d2).wait_send()


def shards(queries, prefix_kv, suffix_kv):
    suf_count, seq, width = queries.shape
    half = width // 2
    rows = (half // D) * seq
    vmem = pl.BlockSpec(memory_space=pltpu.VMEM)
    return pl.pallas_call(
        kernel,
        out_shape=jax.ShapeDtypeStruct((suf_count, seq, half), jnp.bfloat16),
        in_specs=[pl.BlockSpec(memory_space=pl.ANY), vmem, vmem],
        out_specs=vmem,
        scratch_shapes=[
            pltpu.VMEM((2, 4, 4, LINE, 2, BLOCK, D), jnp.bfloat16),
            pltpu.VMEM((seq, half), jnp.bfloat16),
            pltpu.VMEM((D, rows), jnp.bfloat16),
            pltpu.VMEM(suffix_kv.shape[1:], jnp.bfloat16),
            pltpu.VMEM((TOKENS, LANES), jnp.float32),
            pltpu.VMEM((TOKENS, LANES), jnp.float32),
            pltpu.VMEM((TOKENS, LANES), jnp.bfloat16),
            pltpu.VMEM((TOKENS, LANES), jnp.bfloat16),
            pltpu.VMEM((SUB, LANES), jnp.float32),
            pltpu.VMEM((SUB, LANES), jnp.float32),
            pltpu.VMEM((1, LANES), jnp.float32),
            pltpu.VMEM((1, LANES), jnp.float32),
            pltpu.VMEM((1, rows), jnp.float32),
            pltpu.VMEM((SUB, rows), jnp.float32),
            pltpu.VMEM((D, rows), jnp.float32),
            pltpu.SemaphoreType.DMA,
            pltpu.SemaphoreType.DMA((35,)),
            pltpu.SemaphoreType.DMA((4,)),
            pltpu.SemaphoreType.DMA((16,)),
            pltpu.SemaphoreType.DMA((16,)),
        ],
        compiler_params=pltpu.CompilerParams(
            collective_id=0, has_side_effects=True, vmem_limit_bytes=48 * 2**20
        ),
        cost_estimate=pl.CostEstimate(flops=17 * 10**9, bytes_accessed=2 * 2**20, transcendentals=34 * 10**6),
    )(queries, prefix_kv, suffix_kv)


def solution(mesh):
    in_specs = (P("blk", None, None), P(("blk", "split"), None), P("blk", "split", None))
    out_specs = P("blk", None, "split")
    return jax.shard_map(shards, mesh=mesh, in_specs=in_specs, out_specs=out_specs, check_vma=False)
```

```python
import functools
import math

import jax
import jax.numpy as jnp
from jax import lax
from jax.experimental import pallas as pl
from jax.experimental.pallas import tpu as pltpu
from jax.sharding import PartitionSpec as P

MESH = pl.DeviceIdType.MESH
D = 128
SUB = 8
LANES = 256
LINE = 4
BLOCK = 128
TOKENS = 2 * LINE * BLOCK
PIECES = 4
PIECE = TOKENS // PIECES
LOG2E = 1.4426950408889634
NEG = -1e30


def kernel(
    q_hbm, prefix_hbm, suffix_hbm, out_ref,
    kv, q_in, q_t, prefix_ref, suffix_ref, other, s0, s1, p0, p1, x0, x1, c0, c1, m_ref, l_ref, acc,
    in_sem, send_sem, first_sem, line_sem, sib_sem,
):
    scale = LOG2E / math.sqrt(D)
    scores, weights, tops, fixes = (s0, s1), (p0, p1), (x0, x1), (c0, c1)
    tokens_here = suffix_ref.shape[0]
    seq, width = q_in.shape
    heads = width // D
    rows = heads * seq
    units = rows // LANES

    blk, split = lax.axis_index("blk"), lax.axis_index("split")
    core = blk % 2
    x, y, z = blk // 16, (blk // 2) % 4, split * 2 + (blk // 8) % 2

    def device(d1=0, d2=0, d3=0, other_core=0):
        nx = (x + d1 * (1 - core) + d3 * core) % 4
        ny = (y + d2) % 4
        nz = (z + d1 * core + d3 * (1 - core)) % 4
        nc = (core + other_core) % 2
        return (nx * 16 + (nz % 2) * 8 + ny * 2 + nc, nz // 2)

    a1 = x * (1 - core) + z * core
    a3 = z * (1 - core) + x * core
    sibling = device(other_core=1)
    partner = ((x * 16 + (z % 2) * 8 + y * 2 + core), 1 - split)
    copies_here = [device(**{axis: d}) for axis in ("d1", "d2", "d3") for d in (1, 2, 3)]
    copies_here += [device(d3=d, other_core=1) for d in (1, 2, 3)] + [sibling, partner]
    barrier = pltpu.get_barrier_semaphore()
    for peer in copies_here:
        pl.semaphore_signal(barrier, inc=1, device_id=peer, device_id_type=MESH)

    prefix_copy = pltpu.make_async_copy(prefix_hbm, prefix_ref, in_sem.at[0])
    suffix_copy = pltpu.make_async_copy(suffix_hbm.at[0], suffix_ref, in_sem.at[1])
    q_copy = pltpu.make_async_copy(
        q_hbm.at[0, :, pl.ds(pl.multiple_of(split * width, width), width)], q_in, in_sem.at[2]
    )
    prefix_copy.start()
    suffix_copy.start()
    q_copy.start()
    prefix_copy.wait()

    kv[core, a3, y, a1, 0] = prefix_ref[:, :D]
    kv[core, a3, y, a1, 1] = prefix_ref[:, D:].astype(jnp.float32).T.astype(jnp.bfloat16)

    pl.semaphore_wait(barrier, len(copies_here))

    def remote(src, dst, send, recv, target):
        return pltpu.make_async_remote_copy(
            src_ref=src, dst_ref=dst, send_sem=send, recv_sem=recv, device_id=target, device_id_type=MESH
        )

    def first(d, other_core):
        here = kv.at[core, a3, y, a1]
        index = d + 4 * other_core
        return remote(
            here, here, send_sem.at[index], first_sem.at[(4 - d) % 4 + 4 * other_core],
            device(d1=d, other_core=other_core),
        )

    def line_at(d3, d2):
        return kv.at[core, (a3 + d3) % 4, (y + d2) % 4]

    def line_copy(index, d3, d2, s3, s2):
        ref = line_at(d3, d2)
        landing = ((d3 - s3) % 4) * 4 + (d2 - s2) % 4
        return remote(ref, ref, send_sem.at[8 + index], line_sem.at[landing], device(d3=s3 % 4, d2=s2 % 4))

    def sib_copy(d3, d2):
        ref = line_at(d3, d2)
        return remote(ref, ref, send_sem.at[24 + d3 * 4 + d2], sib_sem.at[d3 * 4 + d2], sibling)

    def other_copy():
        return remote(suffix_ref, other, send_sem.at[0], first_sem.at[0], partner)

    plan = [(0, 0, 1, 0), (0, 0, -1, 0), (0, 0, 0, 1), (0, 0, 0, -1), (0, 0, 2, 0), (0, 0, 0, 2)]
    plan += [(0, d2, s3, 0) for d2 in (1, 3, 2) for s3 in (1, -1, 2)]

    def event(d3, d2):
        if (d3, d2) == (0, 0):
            for d in (1, 2, 3):
                first(d, 0).wait_recv()
        else:
            ref = line_at(d3, d2)
            remote(ref, ref, send_sem.at[0], line_sem.at[d3 * 4 + d2], sibling).wait_recv()
        for index, (e3, e2, s3, s2) in enumerate(plan):
            if (e3, e2) == (d3, d2):
                line_copy(index, e3, e2, s3, s2).start()
        if (d3, d2) != (0, 0):
            sib_copy(d3, d2).start()

    def sib_wait(d3, d2):
        if (d3, d2) == (0, 0):
            for d in range(4):
                first(d, 1).wait_recv()
            return
        ref = kv.at[1 - core, (a1 + d3) % 4, (y + d2) % 4]
        remote(ref, ref, send_sem.at[0], sib_sem.at[d3 * 4 + d2], sibling).wait_recv()

    for other_core in (0, 1):
        for d in (1, 3, 2):
            first(d, other_core).start()
    first(0, 1).start()
    suffix_copy.wait()
    other_copy().start()

    m_ref[...] = jnp.full_like(m_ref, NEG)
    l_ref[...] = jnp.zeros_like(l_ref)
    acc[...] = jnp.zeros_like(acc)
    p1[...] = jnp.zeros_like(p1)
    c1[...] = jnp.ones_like(c1)
    q_copy.wait()
    for h in range(heads):
        q_t[:, h * seq : (h + 1) * seq] = q_in[:, h * D : (h + 1) * D].astype(jnp.float32).T.astype(jnp.bfloat16)

    def cols(b):
        return slice(b * LANES, (b + 1) * LANES)

    def tile_max(s):
        return jnp.max(s.reshape(s.shape[0] // SUB, SUB, LANES), axis=0)

    def own_part(keys, values_t, offset):
        for b in range(units):
            s = jnp.dot(keys, q_t[:, cols(b)], preferred_element_type=jnp.float32)
            u = lax.broadcasted_iota(jnp.int32, s.shape, 0) + offset
            t = lax.broadcasted_iota(jnp.int32, s.shape, 1) + (b * LANES) % seq
            s = jnp.where(u <= t, s, NEG)
            m_old = m_ref[:, cols(b)]
            m_new = jnp.maximum(m_old, jnp.max(tile_max(s), axis=0, keepdims=True) * scale)
            fix = jnp.exp2(m_old - m_new)
            m_ref[:, cols(b)] = m_new
            p = jnp.exp2(s * scale - m_new)
            l_ref[:, cols(b)] = l_ref[:, cols(b)] * fix + jnp.sum(p.reshape(-1, SUB, LANES), axis=0)
            acc[:, cols(b)] = acc[:, cols(b)] * fix + jnp.dot(
                values_t, p.astype(jnp.bfloat16), preferred_element_type=jnp.float32
            )

    def values_of(ref):
        return ref[:, D:].astype(jnp.float32).T.astype(jnp.bfloat16)

    own_part(suffix_ref[:, :D], values_of(suffix_ref), split * tokens_here)

    order = [
        ((0, 0, 0), (1, 0, 0)), ((0, 1, 0), (0, 3, 0)), ((1, 1, 0), (1, 3, 0)), ((0, 2, 0), (0, 0, 1)),
        ((0, 0, 3), (1, 2, 0)), ((1, 0, 1), (1, 0, 3)), ((0, 0, 2), (1, 0, 2)), ((0, 1, 1), (0, 3, 1)),
        ((1, 1, 1), (1, 3, 1)), ((0, 1, 3), (0, 3, 3)), ((1, 1, 3), (1, 3, 3)), ((0, 2, 1), (1, 2, 1)),
        ((0, 2, 3), (1, 2, 3)), ((0, 1, 2), (1, 1, 2)), ((0, 3, 2), (1, 3, 2)), ((0, 2, 2), (1, 2, 2)),
    ]

    def packed(k, part, i):
        word = sum(step[k][part] << (2 * at) for at, step in enumerate(order))
        word = word - (1 << 32) if word >= 1 << 31 else word
        return (jnp.int32(word) >> (2 * i)) & 3

    def lines(i):
        found = []
        for k in (0, 1):
            stream, d3, d2 = (packed(k, part, i) for part in range(3))
            base = a3 * (1 - stream) + a1 * stream
            found.append((core + stream * (1 - 2 * core), (base + d3) % 4, (y + d2) % 4))
        return found

    def keys_of(i, j):
        c, l3, l2 = lines(i)[j // 2]
        k = 2 * (j % 2)
        return kv[c, l3, l2, pl.ds(k, 2), 0].reshape(PIECE, D)

    def qk(i, b, buf, j, top):
        s = jnp.dot(keys_of(i, j), q_t[:, cols(b)], preferred_element_type=jnp.float32)
        scores[buf][j * PIECE : (j + 1) * PIECE, :] = s
        here = tile_max(s)
        return here if top is None else jnp.maximum(top, here)

    def pv(i, buf):
        parts = []
        for c, l3, l2 in lines(i):
            parts += [kv[c, l3, l2, k, 1] for k in range(LINE)]
        return jnp.dot(jnp.concatenate(parts, axis=1), weights[buf][...], preferred_element_type=jnp.float32)

    last = 15

    def unit(i, b):
        ni, nb = (i, b + 1) if b < units - 1 else (jnp.minimum(i + 1, last), 0)
        pi, pb = (i, b - 1) if b > 0 else (jnp.maximum(i - 1, 0), units - 1)
        buf, nbuf = b % 2, (b + 1) % 2
        m_old = m_ref[:, cols(b)]
        m_new = jnp.maximum(m_old, jnp.max(tops[buf][...], axis=0, keepdims=True) * scale)
        fix = jnp.exp2(m_old - m_new)
        m_ref[:, cols(b)] = m_new
        fixes[buf][...] = fix
        total = l_ref[:, cols(b)] * fix
        top, add = None, None
        for j in range(PIECES):
            top = qk(ni, nb, nbuf, j, top)
            if j == 0:
                add = pv(pi, nbuf)
            part = slice(j * PIECE, (j + 1) * PIECE)
            p = jnp.exp2(scores[buf][part, :] * scale - m_new)
            weights[buf][part, :] = p.astype(jnp.bfloat16)
            total = total + jnp.sum(p.reshape(-1, SUB, LANES), axis=0)
        tops[nbuf][...] = top
        l_ref[:, cols(b)] = total
        acc[:, cols(pb)] = acc[:, cols(pb)] * fixes[nbuf][...] + add

    handed = {
        (0, 7): [(1, 0), (3, 0)],
        (1, 7): [(0, 1), (0, 3), (2, 0)],
        (3, 4): [(0, 2)],
        (4, 0): [(1, 1), (3, 1)],
        (5, 0): [(1, 3), (3, 3)],
        (6, 0): [(2, 1), (2, 3)],
        (7, 0): [(1, 2), (3, 2)],
        (8, 0): [(2, 2)],
    }

    event(0, 0)
    other_copy().wait_recv()
    own_part(other[:, :D], values_of(other), (1 - split) * tokens_here)
    sib_wait(0, 0)
    top = None
    for j in range(PIECES):
        top = qk(0, 0, 0, j, top)
    tops[0][...] = top

    def body(i, carry):
        for b in range(units):
            for (step, place), group in handed.items():
                if place == b:
                    @pl.when(i == step)
                    def _(group=group):
                        for d3, d2 in group:
                            event(d3, d2)
            if b == units - 1:
                for step in [k for k in range(1, 16) if order[k][0][0] + order[k][1][0]]:
                    @pl.when(i + 1 == step)
                    def _(step=step):
                        for stream, d3, d2 in order[step]:
                            if stream == 1:
                                sib_wait(d3, d2)
            unit(i, b)
        return carry

    lax.fori_loop(0, 16, body, 0)
    pb = units - 1
    acc[:, cols(pb)] = acc[:, cols(pb)] * fixes[pb % 2][...] + pv(last, pb % 2)

    for h in range(heads):
        part = slice(h * seq, (h + 1) * seq)
        inverse = 1.0 / jnp.sum(l_ref[:, part], axis=0, keepdims=True)
        out_ref[0, :, h * D : (h + 1) * D] = (acc[:, part] * inverse).T.astype(jnp.bfloat16)

    for d in (1, 2, 3):
        first(d, 0).wait_send()
    for d in range(4):
        first(d, 1).wait_send()
    other_copy().wait_send()
    for index, (e3, e2, s3, s2) in enumerate(plan):
        line_copy(index, e3, e2, s3, s2).wait_send()
    for d3 in range(4):
        for d2 in range(4):
            if (d3, d2) != (0, 0):
                sib_copy(d3, d2).wait_send()


def shards(queries, prefix_kv, suffix_kv):
    suf_count, seq, width = queries.shape
    half = width // 2
    rows = (half // D) * seq
    vmem = pl.BlockSpec(memory_space=pltpu.VMEM)
    return pl.pallas_call(
        kernel,
        out_shape=jax.ShapeDtypeStruct((suf_count, seq, half), jnp.bfloat16),
        in_specs=[pl.BlockSpec(memory_space=pltpu.HBM)] * 3,
        out_specs=vmem,
        scratch_shapes=[
            pltpu.VMEM((2, 4, 4, LINE, 2, BLOCK, D), jnp.bfloat16),
            pltpu.VMEM((seq, half), jnp.bfloat16),
            pltpu.VMEM((D, rows), jnp.bfloat16),
            pltpu.VMEM(prefix_kv.shape, jnp.bfloat16),
            pltpu.VMEM(suffix_kv.shape[1:], jnp.bfloat16),
            pltpu.VMEM(suffix_kv.shape[1:], jnp.bfloat16),
            pltpu.VMEM((TOKENS, LANES), jnp.float32),
            pltpu.VMEM((TOKENS, LANES), jnp.float32),
            pltpu.VMEM((TOKENS, LANES), jnp.bfloat16),
            pltpu.VMEM((TOKENS, LANES), jnp.bfloat16),
            pltpu.VMEM((SUB, LANES), jnp.float32),
            pltpu.VMEM((SUB, LANES), jnp.float32),
            pltpu.VMEM((1, LANES), jnp.float32),
            pltpu.VMEM((1, LANES), jnp.float32),
            pltpu.VMEM((1, rows), jnp.float32),
            pltpu.VMEM((SUB, rows), jnp.float32),
            pltpu.VMEM((D, rows), jnp.float32),
            pltpu.SemaphoreType.DMA((3,)),
            pltpu.SemaphoreType.DMA((40,)),
            pltpu.SemaphoreType.DMA((8,)),
            pltpu.SemaphoreType.DMA((16,)),
            pltpu.SemaphoreType.DMA((16,)),
        ],
        compiler_params=pltpu.CompilerParams(
            collective_id=0, has_side_effects=True, vmem_limit_bytes=60 * 2**20
        ),
        cost_estimate=pl.CostEstimate(flops=17 * 10**9, bytes_accessed=2 * 2**20, transcendentals=34 * 10**6),
    )(queries, prefix_kv, suffix_kv)


def solution(mesh):
    in_specs = (P("blk", None, None), P(("blk", "split"), None), P("blk", "split", None))
    out_specs = P("blk", None, "split")
    return jax.shard_map(shards, mesh=mesh, in_specs=in_specs, out_specs=out_specs, check_vma=False)
```

```python
import functools
import math

import jax
import jax.numpy as jnp
from jax import lax
from jax.experimental import pallas as pl
from jax.experimental.pallas import tpu as pltpu
from jax.sharding import PartitionSpec as P

MESH = pl.DeviceIdType.MESH
D = 128
SUB = 8
LANES = 256
LINE = 4
BLOCK = 128
TOKENS = 2 * LINE * BLOCK
PIECES = 4
PIECE = TOKENS // PIECES
LOG2E = 1.4426950408889634
NEG = -1e30


def kernel(
    q_hbm, prefix_hbm, suffix_hbm, out_ref,
    kv, q_in, q_t, prefix_ref, suffix_ref, other, s0, s1, p0, p1, x0, x1, c0, c1, m_ref, l_ref, acc,
    in_sem, send_sem, first_sem, line_sem, sib_sem,
):
    scale = LOG2E / math.sqrt(D)
    scores, weights, tops, fixes = (s0, s1), (p0, p1), (x0, x1), (c0, c1)
    tokens_here = suffix_ref.shape[0]
    seq, width = q_in.shape
    heads = width // D
    rows = heads * seq
    units = rows // LANES

    blk, split = lax.axis_index("blk"), lax.axis_index("split")
    core = blk % 2
    x, y, z = blk // 16, (blk // 2) % 4, split * 2 + (blk // 8) % 2

    def device(d1=0, d2=0, d3=0, other_core=0):
        nx = (x + d1 * (1 - core) + d3 * core) % 4
        ny = (y + d2) % 4
        nz = (z + d1 * core + d3 * (1 - core)) % 4
        nc = (core + other_core) % 2
        return (nx * 16 + (nz % 2) * 8 + ny * 2 + nc, nz // 2)

    a1 = x * (1 - core) + z * core
    a3 = z * (1 - core) + x * core
    sibling = device(other_core=1)
    partner = ((x * 16 + (z % 2) * 8 + y * 2 + core), 1 - split)
    copies_here = [device(**{axis: d}) for axis in ("d1", "d2", "d3") for d in (1, 2, 3)]
    copies_here += [device(d3=d, other_core=1) for d in (1, 2, 3)] + [sibling, partner]
    barrier = pltpu.get_barrier_semaphore()
    for peer in copies_here:
        pl.semaphore_signal(barrier, inc=1, device_id=peer, device_id_type=MESH)

    prefix_copy = pltpu.make_async_copy(prefix_hbm, prefix_ref, in_sem.at[0])
    suffix_copy = pltpu.make_async_copy(suffix_hbm.at[0], suffix_ref, in_sem.at[1])
    q_copy = pltpu.make_async_copy(
        q_hbm.at[0, :, pl.ds(pl.multiple_of(split * width, width), width)], q_in, in_sem.at[2]
    )
    prefix_copy.start()
    suffix_copy.start()
    q_copy.start()
    prefix_copy.wait()

    kv[core, a3, y, a1, 0] = prefix_ref[:, :D]
    kv[core, a3, y, a1, 1] = prefix_ref[:, D:].astype(jnp.float32).T.astype(jnp.bfloat16)

    pl.semaphore_wait(barrier, len(copies_here))

    def remote(src, dst, send, recv, target):
        return pltpu.make_async_remote_copy(
            src_ref=src, dst_ref=dst, send_sem=send, recv_sem=recv, device_id=target, device_id_type=MESH
        )

    def first(d, other_core):
        here = kv.at[core, a3, y, a1]
        index = d + 4 * other_core
        return remote(
            here, here, send_sem.at[index], first_sem.at[(4 - d) % 4 + 4 * other_core],
            device(d1=d, other_core=other_core),
        )

    def line_at(d3, d2):
        return kv.at[core, (a3 + d3) % 4, (y + d2) % 4]

    def line_copy(index, d3, d2, s3, s2):
        ref = line_at(d3, d2)
        landing = ((d3 - s3) % 4) * 4 + (d2 - s2) % 4
        return remote(ref, ref, send_sem.at[8 + index], line_sem.at[landing], device(d3=s3 % 4, d2=s2 % 4))

    def sib_copy(d3, d2):
        ref = line_at(d3, d2)
        return remote(ref, ref, send_sem.at[24 + d3 * 4 + d2], sib_sem.at[d3 * 4 + d2], sibling)

    def other_copy():
        return remote(suffix_ref, other, send_sem.at[0], first_sem.at[0], partner)

    plan = [(0, 0, 1, 0), (0, 0, -1, 0), (0, 0, 0, 1), (0, 0, 0, -1), (0, 0, 2, 0), (0, 0, 0, 2)]
    plan += [(0, d2, s3, 0) for d2 in (1, 3, 2) for s3 in (1, -1, 2)]

    def event(d3, d2):
        if (d3, d2) == (0, 0):
            for d in (1, 2, 3):
                first(d, 0).wait_recv()
        else:
            ref = line_at(d3, d2)
            remote(ref, ref, send_sem.at[0], line_sem.at[d3 * 4 + d2], sibling).wait_recv()
        for index, (e3, e2, s3, s2) in enumerate(plan):
            if (e3, e2) == (d3, d2):
                line_copy(index, e3, e2, s3, s2).start()
        if (d3, d2) != (0, 0):
            sib_copy(d3, d2).start()

    def sib_wait(d3, d2):
        if (d3, d2) == (0, 0):
            for d in range(4):
                first(d, 1).wait_recv()
            return
        ref = kv.at[1 - core, (a1 + d3) % 4, (y + d2) % 4]
        remote(ref, ref, send_sem.at[0], sib_sem.at[d3 * 4 + d2], sibling).wait_recv()

    for other_core in (0, 1):
        for d in (1, 3, 2):
            first(d, other_core).start()
    first(0, 1).start()
    suffix_copy.wait()
    other_copy().start()

    m_ref[...] = jnp.full_like(m_ref, NEG)
    l_ref[...] = jnp.zeros_like(l_ref)
    acc[...] = jnp.zeros_like(acc)
    s1[...] = jnp.full_like(s1, NEG)
    x1[...] = jnp.full_like(x1, NEG)
    p0[...] = jnp.zeros_like(p0)
    c0[...] = jnp.ones_like(c0)
    q_copy.wait()
    for h in range(heads):
        q_t[:, h * seq : (h + 1) * seq] = q_in[:, h * D : (h + 1) * D].astype(jnp.float32).T.astype(jnp.bfloat16)

    def cols(b):
        return slice(b * LANES, (b + 1) * LANES)

    def tile_max(s):
        return jnp.max(s.reshape(s.shape[0] // SUB, SUB, LANES), axis=0)

    def own_part(keys, values_t, offset):
        for b in range(units):
            s = jnp.dot(keys, q_t[:, cols(b)], preferred_element_type=jnp.float32)
            u = lax.broadcasted_iota(jnp.int32, s.shape, 0) + offset
            t = lax.broadcasted_iota(jnp.int32, s.shape, 1) + (b * LANES) % seq
            s = jnp.where(u <= t, s, NEG)
            m_old = m_ref[:, cols(b)]
            m_new = jnp.maximum(m_old, jnp.max(tile_max(s), axis=0, keepdims=True) * scale)
            fix = jnp.exp2(m_old - m_new)
            m_ref[:, cols(b)] = m_new
            p = jnp.exp2(s * scale - m_new)
            l_ref[:, cols(b)] = l_ref[:, cols(b)] * fix + jnp.sum(p.reshape(-1, SUB, LANES), axis=0)
            acc[:, cols(b)] = acc[:, cols(b)] * fix + jnp.dot(
                values_t, p.astype(jnp.bfloat16), preferred_element_type=jnp.float32
            )

    def values_of(ref):
        return ref[:, D:].astype(jnp.float32).T.astype(jnp.bfloat16)

    own_part(suffix_ref[:, :D], values_of(suffix_ref), split * tokens_here)

    order = [
        ((0, 0, 0), (1, 0, 0)), ((0, 1, 0), (0, 3, 0)), ((1, 1, 0), (1, 3, 0)), ((0, 2, 0), (0, 0, 1)),
        ((0, 0, 3), (1, 2, 0)), ((1, 0, 1), (1, 0, 3)), ((0, 0, 2), (1, 0, 2)), ((0, 1, 1), (0, 3, 1)),
        ((1, 1, 1), (1, 3, 1)), ((0, 1, 3), (0, 3, 3)), ((1, 1, 3), (1, 3, 3)), ((0, 2, 1), (1, 2, 1)),
        ((0, 2, 3), (1, 2, 3)), ((0, 1, 2), (1, 1, 2)), ((0, 3, 2), (1, 3, 2)), ((0, 2, 2), (1, 2, 2)),
    ]

    def packed(k, part, i):
        word = sum(step[k][part] << (2 * at) for at, step in enumerate(order))
        word = word - (1 << 32) if word >= 1 << 31 else word
        return (jnp.int32(word) >> (2 * i)) & 3

    def lines(i):
        found = []
        for k in (0, 1):
            stream, d3, d2 = (packed(k, part, i) for part in range(3))
            base = a3 * (1 - stream) + a1 * stream
            found.append((core + stream * (1 - 2 * core), (base + d3) % 4, (y + d2) % 4))
        return found

    def keys_of(i, j):
        c, l3, l2 = lines(i)[j // 2]
        k = 2 * (j % 2)
        return kv[c, l3, l2, pl.ds(k, 2), 0].reshape(PIECE, D)

    def qk(i, b, buf, j, top):
        s = jnp.dot(keys_of(i, j), q_t[:, cols(b)], preferred_element_type=jnp.float32)
        scores[buf][j * PIECE : (j + 1) * PIECE, :] = s
        here = tile_max(s)
        return here if top is None else jnp.maximum(top, here)

    def pv(i, buf):
        parts = []
        for c, l3, l2 in lines(i):
            parts += [kv[c, l3, l2, k, 1] for k in range(LINE)]
        return jnp.dot(jnp.concatenate(parts, axis=1), weights[buf][...], preferred_element_type=jnp.float32)

    def softmax_begin(b):
        buf = b % 2
        m_old = m_ref[:, cols(b)]
        m_new = jnp.maximum(m_old, jnp.max(tops[buf][...], axis=0, keepdims=True) * scale)
        fix = jnp.exp2(m_old - m_new)
        m_ref[:, cols(b)] = m_new
        fixes[buf][...] = fix
        return m_new, l_ref[:, cols(b)] * fix

    def softmax_piece(b, j, m_new, total):
        buf = b % 2
        part = slice(j * PIECE, (j + 1) * PIECE)
        p = jnp.exp2(scores[buf][part, :] * scale - m_new)
        weights[buf][part, :] = p.astype(jnp.bfloat16)
        return total + jnp.sum(p.reshape(-1, SUB, LANES), axis=0)

    def unit(i, b):
        b1, b2 = (b - 1) % units, (b - 2) % units
        before = jnp.maximum(i - 1, 0)
        m_new, total = softmax_begin(b1)
        top, add, fix = None, None, None
        for j in range(PIECES):
            top = qk(i, b, b % 2, j, top)
            if j == 0:
                fix = fixes[b % 2][...]
                add = pv(i if b >= 2 else before, b % 2)
            total = softmax_piece(b1, j, m_new, total)
        tops[b % 2][...] = top
        l_ref[:, cols(b1)] = total
        acc[:, cols(b2)] = acc[:, cols(b2)] * fix + add

    handed = {1: [(1, 0), (3, 0)], 3: [(0, 1), (0, 3), (2, 0)], 5: [(0, 2)], 7: [(1, 1), (3, 1), (1, 3), (3, 3)], 9: [(2, 1), (2, 3)], 11: [(1, 2), (3, 2), (2, 2)]}

    event(0, 0)
    other_copy().wait_recv()
    own_part(other[:, :D], values_of(other), (1 - split) * tokens_here)

    def body(i, carry):
        for step in range(16):
            waits = [line[1:] for line in order[step] if line[0] == 1]
            if waits or step in handed:
                @pl.when(i == step)
                def _(step=step, waits=waits):
                    for d3, d2 in handed.get(step, []):
                        event(d3, d2)
                    for d3, d2 in waits:
                        sib_wait(d3, d2)
        for b in range(units):
            unit(i, b)
        return carry

    lax.fori_loop(0, 16, body, 0)
    for b in (units - 2, units - 1):
        if b == units - 1:
            m_new, total = softmax_begin(b)
            for j in range(PIECES):
                total = softmax_piece(b, j, m_new, total)
            l_ref[:, cols(b)] = total
        acc[:, cols(b)] = acc[:, cols(b)] * fixes[b % 2][...] + pv(15, b % 2)

    for h in range(heads):
        part = slice(h * seq, (h + 1) * seq)
        inverse = 1.0 / jnp.sum(l_ref[:, part], axis=0, keepdims=True)
        out_ref[0, :, h * D : (h + 1) * D] = (acc[:, part] * inverse).T.astype(jnp.bfloat16)

    for d in (1, 2, 3):
        first(d, 0).wait_send()
    for d in range(4):
        first(d, 1).wait_send()
    other_copy().wait_send()
    for index, (e3, e2, s3, s2) in enumerate(plan):
        line_copy(index, e3, e2, s3, s2).wait_send()
    for d3 in range(4):
        for d2 in range(4):
            if (d3, d2) != (0, 0):
                sib_copy(d3, d2).wait_send()


def shards(queries, prefix_kv, suffix_kv):
    suf_count, seq, width = queries.shape
    half = width // 2
    rows = (half // D) * seq
    vmem = pl.BlockSpec(memory_space=pltpu.VMEM)
    return pl.pallas_call(
        kernel,
        out_shape=jax.ShapeDtypeStruct((suf_count, seq, half), jnp.bfloat16),
        in_specs=[pl.BlockSpec(memory_space=pltpu.HBM)] * 3,
        out_specs=vmem,
        scratch_shapes=[
            pltpu.VMEM((2, 4, 4, LINE, 2, BLOCK, D), jnp.bfloat16),
            pltpu.VMEM((seq, half), jnp.bfloat16),
            pltpu.VMEM((D, rows), jnp.bfloat16),
            pltpu.VMEM(prefix_kv.shape, jnp.bfloat16),
            pltpu.VMEM(suffix_kv.shape[1:], jnp.bfloat16),
            pltpu.VMEM(suffix_kv.shape[1:], jnp.bfloat16),
            pltpu.VMEM((TOKENS, LANES), jnp.float32),
            pltpu.VMEM((TOKENS, LANES), jnp.float32),
            pltpu.VMEM((TOKENS, LANES), jnp.bfloat16),
            pltpu.VMEM((TOKENS, LANES), jnp.bfloat16),
            pltpu.VMEM((SUB, LANES), jnp.float32),
            pltpu.VMEM((SUB, LANES), jnp.float32),
            pltpu.VMEM((1, LANES), jnp.float32),
            pltpu.VMEM((1, LANES), jnp.float32),
            pltpu.VMEM((1, rows), jnp.float32),
            pltpu.VMEM((SUB, rows), jnp.float32),
            pltpu.VMEM((D, rows), jnp.float32),
            pltpu.SemaphoreType.DMA((3,)),
            pltpu.SemaphoreType.DMA((40,)),
            pltpu.SemaphoreType.DMA((8,)),
            pltpu.SemaphoreType.DMA((16,)),
            pltpu.SemaphoreType.DMA((16,)),
        ],
        compiler_params=pltpu.CompilerParams(
            collective_id=0, has_side_effects=True, vmem_limit_bytes=60 * 2**20
        ),
        cost_estimate=pl.CostEstimate(flops=17 * 10**9, bytes_accessed=2 * 2**20, transcendentals=34 * 10**6),
    )(queries, prefix_kv, suffix_kv)


def solution(mesh):
    in_specs = (P("blk", None, None), P(("blk", "split"), None), P("blk", "split", None))
    out_specs = P("blk", None, "split")
    return jax.shard_map(shards, mesh=mesh, in_specs=in_specs, out_specs=out_specs, check_vma=False)
```

```python
import functools
import math

import jax
import jax.numpy as jnp
from jax import lax
from jax.experimental import pallas as pl
from jax.experimental.pallas import tpu as pltpu
from jax.sharding import PartitionSpec as P

MESH = pl.DeviceIdType.MESH
D = 128
SUB = 8
LANES = 256
LINE = 4
BLOCK = 128
TOKENS = 2 * LINE * BLOCK
PIECES = 4
PIECE = TOKENS // PIECES
LOG2E = 1.4426950408889634
NEG = -1e30


def kernel(
    q_hbm, prefix_hbm, suffix_hbm, out_ref,
    kv, q_in, q_t, prefix_ref, suffix_ref, other, s0, s1, x0, x1, m_ref, l_ref, acc,
    in_sem, send_sem, first_sem, line_sem, sib_sem,
):
    scale = LOG2E / math.sqrt(D)
    scores, tops = (s0, s1), (x0, x1)
    tokens_here = suffix_ref.shape[0]
    seq, width = q_in.shape
    heads = width // D
    rows = heads * seq
    units = rows // LANES

    blk, split = lax.axis_index("blk"), lax.axis_index("split")
    core = blk % 2
    x, y, z = blk // 16, (blk // 2) % 4, split * 2 + (blk // 8) % 2

    def device(d1=0, d2=0, d3=0, other_core=0):
        nx = (x + d1 * (1 - core) + d3 * core) % 4
        ny = (y + d2) % 4
        nz = (z + d1 * core + d3 * (1 - core)) % 4
        nc = (core + other_core) % 2
        return (nx * 16 + (nz % 2) * 8 + ny * 2 + nc, nz // 2)

    a1 = x * (1 - core) + z * core
    a3 = z * (1 - core) + x * core
    sibling = device(other_core=1)
    partner = ((x * 16 + (z % 2) * 8 + y * 2 + core), 1 - split)
    copies_here = [device(**{axis: d}) for axis in ("d1", "d2", "d3") for d in (1, 2, 3)]
    copies_here += [device(d3=d, other_core=1) for d in (1, 2, 3)] + [sibling, partner]
    barrier = pltpu.get_barrier_semaphore()
    for peer in copies_here:
        pl.semaphore_signal(barrier, inc=1, device_id=peer, device_id_type=MESH)

    prefix_copy = pltpu.make_async_copy(prefix_hbm, prefix_ref, in_sem.at[0])
    suffix_copy = pltpu.make_async_copy(suffix_hbm.at[0], suffix_ref, in_sem.at[1])
    q_copy = pltpu.make_async_copy(
        q_hbm.at[0, :, pl.ds(pl.multiple_of(split * width, width), width)], q_in, in_sem.at[2]
    )
    prefix_copy.start()
    suffix_copy.start()
    q_copy.start()
    prefix_copy.wait()

    own_line = core * 16 + a3 * 4 + y
    kv[own_line, a1, 0] = prefix_ref[:, :D]
    kv[own_line, a1, 1] = prefix_ref[:, D:].astype(jnp.float32).T.astype(jnp.bfloat16)

    pl.semaphore_wait(barrier, len(copies_here))

    def remote(src, dst, send, recv, target):
        return pltpu.make_async_remote_copy(
            src_ref=src, dst_ref=dst, send_sem=send, recv_sem=recv, device_id=target, device_id_type=MESH
        )

    def first(d, other_core):
        here = kv.at[own_line, a1]
        index = d + 4 * other_core
        return remote(
            here, here, send_sem.at[index], first_sem.at[(4 - d) % 4 + 4 * other_core],
            device(d1=d, other_core=other_core),
        )

    def line_at(d3, d2):
        return kv.at[core * 16 + (a3 + d3) % 4 * 4 + (y + d2) % 4]

    def line_copy(index, d3, d2, s3, s2):
        ref = line_at(d3, d2)
        landing = ((d3 - s3) % 4) * 4 + (d2 - s2) % 4
        return remote(ref, ref, send_sem.at[8 + index], line_sem.at[landing], device(d3=s3 % 4, d2=s2 % 4))

    def sib_copy(d3, d2):
        ref = line_at(d3, d2)
        return remote(ref, ref, send_sem.at[24 + d3 * 4 + d2], sib_sem.at[d3 * 4 + d2], sibling)

    def other_copy():
        return remote(suffix_ref, other, send_sem.at[0], first_sem.at[0], partner)

    plan = [(0, 0, 1, 0), (0, 0, -1, 0), (0, 0, 0, 1), (0, 0, 0, -1), (0, 0, 2, 0), (0, 0, 0, 2)]
    plan += [(0, d2, s3, 0) for d2 in (1, 3, 2) for s3 in (1, -1, 2)]

    def event(d3, d2):
        if (d3, d2) == (0, 0):
            for d in (1, 2, 3):
                first(d, 0).wait_recv()
        else:
            ref = line_at(d3, d2)
            remote(ref, ref, send_sem.at[0], line_sem.at[d3 * 4 + d2], sibling).wait_recv()
        for index, (e3, e2, s3, s2) in enumerate(plan):
            if (e3, e2) == (d3, d2):
                line_copy(index, e3, e2, s3, s2).start()
        if (d3, d2) != (0, 0):
            sib_copy(d3, d2).start()

    def sib_wait(d3, d2):
        if (d3, d2) == (0, 0):
            for d in range(4):
                first(d, 1).wait_recv()
            return
        ref = kv.at[(1 - core) * 16 + (a1 + d3) % 4 * 4 + (y + d2) % 4]
        remote(ref, ref, send_sem.at[0], sib_sem.at[d3 * 4 + d2], sibling).wait_recv()

    for other_core in (0, 1):
        for d in (1, 3, 2):
            first(d, other_core).start()
    first(0, 1).start()
    suffix_copy.wait()
    other_copy().start()

    m_ref[...] = jnp.full_like(m_ref, NEG)
    l_ref[...] = jnp.zeros_like(l_ref)
    acc[...] = jnp.zeros_like(acc)
    s1[...] = jnp.full_like(s1, NEG)
    x1[...] = jnp.full_like(x1, NEG)
    q_copy.wait()
    for h in range(heads):
        q_t[:, h * seq : (h + 1) * seq] = q_in[:, h * D : (h + 1) * D].astype(jnp.float32).T.astype(jnp.bfloat16)

    def cols(b):
        return slice(b * LANES, (b + 1) * LANES)

    def tile_max(s):
        return jnp.max(s.reshape(s.shape[0] // SUB, SUB, LANES), axis=0)

    def own_part(keys, values_t, offset):
        for b in range(units):
            s = jnp.dot(keys, q_t[:, cols(b)], preferred_element_type=jnp.float32)
            u = lax.broadcasted_iota(jnp.int32, s.shape, 0) + offset
            t = lax.broadcasted_iota(jnp.int32, s.shape, 1) + (b * LANES) % seq
            s = jnp.where(u <= t, s, NEG)
            m_old = m_ref[:, cols(b)]
            m_new = jnp.maximum(m_old, jnp.max(tile_max(s), axis=0, keepdims=True) * scale)
            fix = jnp.exp2(m_old - m_new)
            m_ref[:, cols(b)] = m_new
            p = jnp.exp2(s * scale - m_new)
            l_ref[:, cols(b)] = l_ref[:, cols(b)] * fix + jnp.sum(p.reshape(-1, SUB, LANES), axis=0)
            acc[:, cols(b)] = acc[:, cols(b)] * fix + jnp.dot(
                values_t, p.astype(jnp.bfloat16), preferred_element_type=jnp.float32
            )

    def values_of(ref):
        return ref[:, D:].astype(jnp.float32).T.astype(jnp.bfloat16)

    own_part(suffix_ref[:, :D], values_of(suffix_ref), split * tokens_here)

    order = [
        ((0, 0, 0), (1, 0, 0)), ((0, 1, 0), (0, 3, 0)), ((1, 1, 0), (1, 3, 0)), ((0, 2, 0), (0, 0, 1)),
        ((0, 0, 3), (1, 2, 0)), ((1, 0, 1), (1, 0, 3)), ((0, 0, 2), (1, 0, 2)), ((0, 1, 1), (0, 3, 1)),
        ((1, 1, 1), (1, 3, 1)), ((0, 1, 3), (0, 3, 3)), ((1, 1, 3), (1, 3, 3)), ((0, 2, 1), (1, 2, 1)),
        ((0, 2, 3), (1, 2, 3)), ((0, 1, 2), (1, 1, 2)), ((0, 3, 2), (1, 3, 2)), ((0, 2, 2), (1, 2, 2)),
    ]

    def packed(k, part, i):
        word = sum(step[k][part] << (2 * at) for at, step in enumerate(order))
        word = word - (1 << 32) if word >= 1 << 31 else word
        return (jnp.int32(word) >> (2 * i)) & 3

    def lines(i):
        found = []
        for k in (0, 1):
            stream, d3, d2 = (packed(k, part, i) for part in range(3))
            base = a3 * (1 - stream) + a1 * stream
            found.append((core + stream * (1 - 2 * core)) * 16 + ((base + d3) & 3) * 4 + ((y + d2) & 3))
        return found

    def keys_of(pair, j):
        k = 2 * (j % 2)
        return kv[pair[j // 2], k : k + 2, 0].reshape(PIECE, D)

    def qk(pair, b, buf, j, top):
        s = jnp.dot(keys_of(pair, j), q_t[:, cols(b)], preferred_element_type=jnp.float32)
        scores[buf][j * PIECE : (j + 1) * PIECE, :] = s
        here = tile_max(s)
        return here if top is None else jnp.maximum(top, here)

    def values_piece(pair, j):
        k = 2 * (j % 2)
        return jnp.concatenate([kv[pair[j // 2], k, 1], kv[pair[j // 2], k + 1, 1]], axis=1)

    def unit(pair, before, b):
        b1 = (b - 1) % units
        buf, buf1 = b % 2, (b - 1) % 2
        values_pair = before if b == 0 else pair
        m_new, fix, total = softmax_begin(b1)
        top, add = None, None
        for j in range(PIECES):
            p, total = softmax_piece(b1, j, m_new, total)
            top = qk(pair, b, buf, j, top)
            here = jnp.dot(values_piece(values_pair, j), p, preferred_element_type=jnp.float32)
            add = here if add is None else add + here
        tops[buf][...] = top
        softmax_end(b1, fix, total, add)

    def softmax_begin(b):
        m_old = m_ref[:, cols(b)]
        m_new = jnp.maximum(m_old, jnp.max(tops[b % 2][...], axis=0, keepdims=True) * scale)
        fix = jnp.exp2(m_old - m_new)
        m_ref[:, cols(b)] = m_new
        return m_new, fix, l_ref[:, cols(b)] * fix

    def softmax_piece(b, j, m_new, total):
        p = jnp.exp2(scores[b % 2][j * PIECE : (j + 1) * PIECE, :] * scale - m_new)
        return p.astype(jnp.bfloat16), total + jnp.sum(p.reshape(-1, SUB, LANES), axis=0)

    def softmax_end(b, fix, total, add):
        l_ref[:, cols(b)] = total
        acc[:, cols(b)] = acc[:, cols(b)] * fix + add

    handed = {1: [(1, 0), (3, 0)], 3: [(0, 1), (0, 3), (2, 0)], 5: [(0, 2)], 7: [(1, 1), (3, 1), (1, 3), (3, 3)], 9: [(2, 1), (2, 3)], 11: [(1, 2), (3, 2), (2, 2)]}

    event(0, 0)

    def body(i, carry):
        for step in range(16):
            waits = [line[1:] for line in order[step] if line[0] == 1]
            if waits or step in handed:
                @pl.when(i == step)
                def _(step=step, waits=waits):
                    if step == 1:
                        other_copy().wait_recv()
                        own_part(other[:, :D], values_of(other), (1 - split) * tokens_here)
                    for d3, d2 in handed.get(step, []):
                        event(d3, d2)
                    for d3, d2 in waits:
                        sib_wait(d3, d2)
        pair, before = lines(i), lines(jnp.maximum(i - 1, 0))
        for b in range(units):
            unit(pair, before, b)
        return carry

    lax.fori_loop(0, 16, body, 0)
    b = units - 1
    m_new, fix, total = softmax_begin(b)
    add = None
    for j in range(PIECES):
        p, total = softmax_piece(b, j, m_new, total)
        here = jnp.dot(values_piece(lines(15), j), p, preferred_element_type=jnp.float32)
        add = here if add is None else add + here
    softmax_end(b, fix, total, add)

    for h in range(heads):
        part = slice(h * seq, (h + 1) * seq)
        inverse = 1.0 / jnp.sum(l_ref[:, part], axis=0, keepdims=True)
        out_ref[0, :, h * D : (h + 1) * D] = (acc[:, part] * inverse).T.astype(jnp.bfloat16)

    for d in (1, 2, 3):
        first(d, 0).wait_send()
    for d in range(4):
        first(d, 1).wait_send()
    other_copy().wait_send()
    for index, (e3, e2, s3, s2) in enumerate(plan):
        line_copy(index, e3, e2, s3, s2).wait_send()
    for d3 in range(4):
        for d2 in range(4):
            if (d3, d2) != (0, 0):
                sib_copy(d3, d2).wait_send()


def shards(queries, prefix_kv, suffix_kv):
    suf_count, seq, width = queries.shape
    half = width // 2
    rows = (half // D) * seq
    vmem = pl.BlockSpec(memory_space=pltpu.VMEM)
    return pl.pallas_call(
        kernel,
        out_shape=jax.ShapeDtypeStruct((suf_count, seq, half), jnp.bfloat16),
        in_specs=[pl.BlockSpec(memory_space=pltpu.HBM)] * 3,
        out_specs=vmem,
        scratch_shapes=[
            pltpu.VMEM((32, LINE, 2, BLOCK, D), jnp.bfloat16),
            pltpu.VMEM((seq, half), jnp.bfloat16),
            pltpu.VMEM((D, rows), jnp.bfloat16),
            pltpu.VMEM(prefix_kv.shape, jnp.bfloat16),
            pltpu.VMEM(suffix_kv.shape[1:], jnp.bfloat16),
            pltpu.VMEM(suffix_kv.shape[1:], jnp.bfloat16),
            pltpu.VMEM((TOKENS, LANES), jnp.float32),
            pltpu.VMEM((TOKENS, LANES), jnp.float32),
            pltpu.VMEM((SUB, LANES), jnp.float32),
            pltpu.VMEM((SUB, LANES), jnp.float32),
            pltpu.VMEM((1, rows), jnp.float32),
            pltpu.VMEM((SUB, rows), jnp.float32),
            pltpu.VMEM((D, rows), jnp.float32),
            pltpu.SemaphoreType.DMA((3,)),
            pltpu.SemaphoreType.DMA((40,)),
            pltpu.SemaphoreType.DMA((8,)),
            pltpu.SemaphoreType.DMA((16,)),
            pltpu.SemaphoreType.DMA((16,)),
        ],
        compiler_params=pltpu.CompilerParams(
            collective_id=0, has_side_effects=True, vmem_limit_bytes=60 * 2**20
        ),
        cost_estimate=pl.CostEstimate(flops=17 * 10**9, bytes_accessed=2 * 2**20, transcendentals=34 * 10**6),
    )(queries, prefix_kv, suffix_kv)


def solution(mesh):
    in_specs = (P("blk", None, None), P(("blk", "split"), None), P("blk", "split", None))
    out_specs = P("blk", None, "split")
    return jax.shard_map(shards, mesh=mesh, in_specs=in_specs, out_specs=out_specs, check_vma=False)
```

```python
import functools
import math

import jax
import jax.numpy as jnp
from jax import lax
from jax.experimental import pallas as pl
from jax.experimental.pallas import tpu as pltpu
from jax.sharding import PartitionSpec as P

MESH = pl.DeviceIdType.MESH
D = 128
SUB = 8
LANES = 256
LINE = 4
BLOCK = 128
TOKENS = 2 * LINE * BLOCK
PIECES = 4
PIECE = TOKENS // PIECES
LOG2E = 1.4426950408889634
NEG = -1e30


def kernel(
    q_hbm, prefix_hbm, suffix_hbm, out_ref,
    kv, q_in, q_t, prefix_ref, suffix_ref, other, s0, s1, x0, x1, m_ref, l_ref, acc,
    in_sem, send_sem, first_sem, line_sem, sib_sem,
):
    scale = LOG2E / math.sqrt(D)
    scores, tops = (s0, s1), (x0, x1)
    tokens_here = suffix_ref.shape[0]
    seq, width = q_in.shape
    heads = width // D
    rows = heads * seq
    units = rows // LANES

    blk, split = lax.axis_index("blk"), lax.axis_index("split")
    core = blk % 2
    x, y, z = blk // 16, (blk // 2) % 4, split * 2 + (blk // 8) % 2

    def device(d1=0, d2=0, d3=0, other_core=0):
        nx = (x + d1 * (1 - core) + d3 * core) % 4
        ny = (y + d2) % 4
        nz = (z + d1 * core + d3 * (1 - core)) % 4
        nc = (core + other_core) % 2
        return (nx * 16 + (nz % 2) * 8 + ny * 2 + nc, nz // 2)

    a1 = x * (1 - core) + z * core
    a3 = z * (1 - core) + x * core
    sibling = device(other_core=1)
    partner = ((x * 16 + (z % 2) * 8 + y * 2 + core), 1 - split)
    prefix_copy = pltpu.make_async_copy(prefix_hbm, prefix_ref, in_sem.at[0])
    suffix_copy = pltpu.make_async_copy(suffix_hbm.at[0], suffix_ref, in_sem.at[1])
    q_copy = pltpu.make_async_copy(
        q_hbm.at[0, :, pl.ds(pl.multiple_of(split * width, width), width)], q_in, in_sem.at[2]
    )
    prefix_copy.start()
    suffix_copy.start()
    q_copy.start()
    copies_here = [device(**{axis: d}) for axis in ("d1", "d2", "d3") for d in (1, 2, 3)]
    copies_here += [device(d3=d, other_core=1) for d in (1, 2, 3)] + [sibling, partner]
    barrier = pltpu.get_barrier_semaphore()
    for peer in copies_here:
        pl.semaphore_signal(barrier, inc=1, device_id=peer, device_id_type=MESH)

    prefix_copy.wait()

    own_line = core * 16 + a3 * 4 + y
    kv[own_line, a1, 0] = prefix_ref[:, :D]
    kv[own_line, a1, 1] = prefix_ref[:, D:].astype(jnp.float32).T.astype(jnp.bfloat16)

    pl.semaphore_wait(barrier, len(copies_here))

    def remote(src, dst, send, recv, target):
        return pltpu.make_async_remote_copy(
            src_ref=src, dst_ref=dst, send_sem=send, recv_sem=recv, device_id=target, device_id_type=MESH
        )

    def first(d, other_core):
        here = kv.at[own_line, a1]
        index = d + 4 * other_core
        return remote(
            here, here, send_sem.at[index], first_sem.at[(4 - d) % 4 + 4 * other_core],
            device(d1=d, other_core=other_core),
        )

    def line_at(d3, d2):
        return kv.at[core * 16 + (a3 + d3) % 4 * 4 + (y + d2) % 4]

    def line_copy(index, d3, d2, s3, s2):
        ref = line_at(d3, d2)
        landing = ((d3 - s3) % 4) * 4 + (d2 - s2) % 4
        return remote(ref, ref, send_sem.at[8 + index], line_sem.at[landing], device(d3=s3 % 4, d2=s2 % 4))

    def sib_copy(d3, d2):
        ref = line_at(d3, d2)
        return remote(ref, ref, send_sem.at[24 + d3 * 4 + d2], sib_sem.at[d3 * 4 + d2], sibling)

    def other_copy():
        return remote(suffix_ref, other, send_sem.at[0], first_sem.at[0], partner)

    plan = [(0, 0, 1, 0), (0, 0, -1, 0), (0, 0, 0, 1), (0, 0, 0, -1), (0, 0, 2, 0), (0, 0, 0, 2)]
    plan += [(0, d2, s3, 0) for d2 in (1, 3, 2) for s3 in (1, -1, 2)]

    def event(d3, d2):
        if (d3, d2) == (0, 0):
            for d in (1, 2, 3):
                first(d, 0).wait_recv()
        else:
            ref = line_at(d3, d2)
            remote(ref, ref, send_sem.at[0], line_sem.at[d3 * 4 + d2], sibling).wait_recv()
        for index, (e3, e2, s3, s2) in enumerate(plan):
            if (e3, e2) == (d3, d2):
                line_copy(index, e3, e2, s3, s2).start()
        if (d3, d2) != (0, 0):
            sib_copy(d3, d2).start()

    def sib_wait(d3, d2):
        if (d3, d2) == (0, 0):
            for d in range(4):
                first(d, 1).wait_recv()
            return
        ref = kv.at[(1 - core) * 16 + (a1 + d3) % 4 * 4 + (y + d2) % 4]
        remote(ref, ref, send_sem.at[0], sib_sem.at[d3 * 4 + d2], sibling).wait_recv()

    for other_core in (0, 1):
        for d in (1, 3, 2):
            first(d, other_core).start()
    first(0, 1).start()
    suffix_copy.wait()
    other_copy().start()

    m_ref[...] = jnp.full_like(m_ref, NEG)
    l_ref[...] = jnp.zeros_like(l_ref)
    acc[...] = jnp.zeros_like(acc)
    s1[...] = jnp.full_like(s1, NEG)
    x1[...] = jnp.full_like(x1, NEG)
    q_copy.wait()
    for h in range(heads):
        q_t[:, h * seq : (h + 1) * seq] = q_in[:, h * D : (h + 1) * D].astype(jnp.float32).T.astype(jnp.bfloat16)

    def cols(b):
        return slice(b * LANES, (b + 1) * LANES)

    def tile_max(s):
        return jnp.max(s.reshape(s.shape[0] // SUB, SUB, LANES), axis=0)

    def own_part(keys, values_t, offset):
        late = [b for b in range(units) if (b * LANES) % seq + LANES > tokens_here]
        own_blocks(late, keys, values_t, offset)

        @pl.when(offset == 0)
        def _():
            own_blocks([b for b in range(units) if b not in late], keys, values_t, offset)

    def own_blocks(blocks, keys, values_t, offset):
        for b in blocks:
            s = jnp.dot(keys, q_t[:, cols(b)], preferred_element_type=jnp.float32)
            u = lax.broadcasted_iota(jnp.int32, s.shape, 0) + offset
            t = lax.broadcasted_iota(jnp.int32, s.shape, 1) + (b * LANES) % seq
            s = jnp.where(u <= t, s, NEG)
            m_old = m_ref[:, cols(b)]
            m_new = jnp.maximum(m_old, jnp.max(tile_max(s), axis=0, keepdims=True) * scale)
            fix = jnp.exp2(m_old - m_new)
            m_ref[:, cols(b)] = m_new
            p = jnp.exp2(s * scale - m_new)
            l_ref[:, cols(b)] = l_ref[:, cols(b)] * fix + jnp.sum(p.reshape(-1, SUB, LANES), axis=0)
            acc[:, cols(b)] = acc[:, cols(b)] * fix + jnp.dot(
                values_t, p.astype(jnp.bfloat16), preferred_element_type=jnp.float32
            )

    def values_of(ref):
        return ref[:, D:].astype(jnp.float32).T.astype(jnp.bfloat16)

    own_part(suffix_ref[:, :D], values_of(suffix_ref), split * tokens_here)

    order = [
        ((0, 0, 0), (1, 0, 0)), ((0, 1, 0), (0, 3, 0)), ((1, 1, 0), (1, 3, 0)), ((0, 2, 0), (0, 0, 1)),
        ((0, 0, 3), (1, 2, 0)), ((1, 0, 1), (1, 0, 3)), ((0, 0, 2), (1, 0, 2)), ((0, 1, 1), (0, 3, 1)),
        ((1, 1, 1), (1, 3, 1)), ((0, 1, 3), (0, 3, 3)), ((1, 1, 3), (1, 3, 3)), ((0, 2, 1), (1, 2, 1)),
        ((0, 2, 3), (1, 2, 3)), ((0, 1, 2), (1, 1, 2)), ((0, 3, 2), (1, 3, 2)), ((0, 2, 2), (1, 2, 2)),
    ]

    def packed(k, part, i):
        word = sum(step[k][part] << (2 * at) for at, step in enumerate(order))
        word = word - (1 << 32) if word >= 1 << 31 else word
        return (jnp.int32(word) >> (2 * i)) & 3

    def lines(i):
        found = []
        for k in (0, 1):
            stream, d3, d2 = (packed(k, part, i) for part in range(3))
            base = a3 * (1 - stream) + a1 * stream
            found.append((core + stream * (1 - 2 * core)) * 16 + ((base + d3) & 3) * 4 + ((y + d2) & 3))
        return found

    def keys_of(pair, j):
        k = 2 * (j % 2)
        return kv[pair[j // 2], k : k + 2, 0].reshape(PIECE, D)

    def qk(pair, b, buf, j, top):
        s = jnp.dot(keys_of(pair, j), q_t[:, cols(b)], preferred_element_type=jnp.float32)
        scores[buf][j * PIECE : (j + 1) * PIECE, :] = s
        here = tile_max(s)
        return here if top is None else jnp.maximum(top, here)

    def values_piece(pair, j):
        k = 2 * (j % 2)
        return jnp.concatenate([kv[pair[j // 2], k, 1], kv[pair[j // 2], k + 1, 1]], axis=1)

    def unit(pair, before, b):
        b1 = (b - 1) % units
        buf, buf1 = b % 2, (b - 1) % 2
        values_pair = before if b == 0 else pair
        m_new, fix, total = softmax_begin(b1)
        top, add = None, None
        for j in range(PIECES):
            p, total = softmax_piece(b1, j, m_new, total)
            top = qk(pair, b, buf, j, top)
            here = jnp.dot(values_piece(values_pair, j), p, preferred_element_type=jnp.float32)
            add = here if add is None else add + here
        tops[buf][...] = top
        softmax_end(b1, fix, total, add)

    def softmax_begin(b):
        m_old = m_ref[:, cols(b)]
        m_new = jnp.maximum(m_old, jnp.max(tops[b % 2][...], axis=0, keepdims=True) * scale)
        fix = jnp.exp2(m_old - m_new)
        m_ref[:, cols(b)] = m_new
        return m_new, fix, l_ref[:, cols(b)] * fix

    def softmax_piece(b, j, m_new, total):
        p = jnp.exp2(scores[b % 2][j * PIECE : (j + 1) * PIECE, :] * scale - m_new)
        return p.astype(jnp.bfloat16), total + jnp.sum(p.reshape(-1, SUB, LANES), axis=0)

    def softmax_end(b, fix, total, add):
        l_ref[:, cols(b)] = total
        acc[:, cols(b)] = acc[:, cols(b)] * fix + add

    handed = {1: [(1, 0), (3, 0)], 3: [(0, 1), (0, 3), (2, 0)], 5: [(0, 2)], 6: [(1, 1), (3, 1)], 8: [(1, 3), (3, 3)], 9: [(2, 1), (2, 3)], 11: [(1, 2), (3, 2)], 13: [(2, 2)]}

    event(0, 0)

    def body(i, carry):
        for step in range(16):
            waits = [line[1:] for line in order[step] if line[0] == 1]
            if waits or step in handed:
                @pl.when(i == step)
                def _(step=step, waits=waits):
                    if step == 1:
                        other_copy().wait_recv()
                        own_part(other[:, :D], values_of(other), (1 - split) * tokens_here)
                    for d3, d2 in handed.get(step, []):
                        event(d3, d2)
                    for d3, d2 in waits:
                        sib_wait(d3, d2)
        pair, before = lines(i), lines(jnp.maximum(i - 1, 0))
        for b in range(units):
            unit(pair, before, b)
        return carry

    lax.fori_loop(0, 16, body, 0)
    b = units - 1
    m_new, fix, total = softmax_begin(b)
    add = None
    for j in range(PIECES):
        p, total = softmax_piece(b, j, m_new, total)
        here = jnp.dot(values_piece(lines(15), j), p, preferred_element_type=jnp.float32)
        add = here if add is None else add + here
    softmax_end(b, fix, total, add)

    for h in range(heads):
        part = slice(h * seq, (h + 1) * seq)
        inverse = 1.0 / jnp.sum(l_ref[:, part], axis=0, keepdims=True)
        out_ref[0, :, h * D : (h + 1) * D] = (acc[:, part] * inverse).T.astype(jnp.bfloat16)

    for d in (1, 2, 3):
        first(d, 0).wait_send()
    for d in range(4):
        first(d, 1).wait_send()
    other_copy().wait_send()
    for index, (e3, e2, s3, s2) in enumerate(plan):
        line_copy(index, e3, e2, s3, s2).wait_send()
    for d3 in range(4):
        for d2 in range(4):
            if (d3, d2) != (0, 0):
                sib_copy(d3, d2).wait_send()


def shards(queries, prefix_kv, suffix_kv):
    suf_count, seq, width = queries.shape
    half = width // 2
    rows = (half // D) * seq
    vmem = pl.BlockSpec(memory_space=pltpu.VMEM)
    return pl.pallas_call(
        kernel,
        out_shape=jax.ShapeDtypeStruct((suf_count, seq, half), jnp.bfloat16),
        in_specs=[pl.BlockSpec(memory_space=pltpu.HBM)] * 3,
        out_specs=vmem,
        scratch_shapes=[
            pltpu.VMEM((32, LINE, 2, BLOCK, D), jnp.bfloat16),
            pltpu.VMEM((seq, half), jnp.bfloat16),
            pltpu.VMEM((D, rows), jnp.bfloat16),
            pltpu.VMEM(prefix_kv.shape, jnp.bfloat16),
            pltpu.VMEM(suffix_kv.shape[1:], jnp.bfloat16),
            pltpu.VMEM(suffix_kv.shape[1:], jnp.bfloat16),
            pltpu.VMEM((TOKENS, LANES), jnp.float32),
            pltpu.VMEM((TOKENS, LANES), jnp.float32),
            pltpu.VMEM((SUB, LANES), jnp.float32),
            pltpu.VMEM((SUB, LANES), jnp.float32),
            pltpu.VMEM((1, rows), jnp.float32),
            pltpu.VMEM((SUB, rows), jnp.float32),
            pltpu.VMEM((D, rows), jnp.float32),
            pltpu.SemaphoreType.DMA((3,)),
            pltpu.SemaphoreType.DMA((40,)),
            pltpu.SemaphoreType.DMA((8,)),
            pltpu.SemaphoreType.DMA((16,)),
            pltpu.SemaphoreType.DMA((16,)),
        ],
        compiler_params=pltpu.CompilerParams(
            collective_id=0, has_side_effects=True, vmem_limit_bytes=60 * 2**20
        ),
        cost_estimate=pl.CostEstimate(flops=17 * 10**9, bytes_accessed=2 * 2**20, transcendentals=34 * 10**6),
    )(queries, prefix_kv, suffix_kv)


def solution(mesh):
    in_specs = (P("blk", None, None), P(("blk", "split"), None), P("blk", "split", None))
    out_specs = P("blk", None, "split")
    return jax.shard_map(shards, mesh=mesh, in_specs=in_specs, out_specs=out_specs, check_vma=False)
```
